32 devices in a mesh: group: 4 (over y, x), inner: 8 (over z, core).
Axes of the slice: x: 2, y: 2, z: 4, core: 2. Of those that a mesh axis runs over, the one named last changes fastest.
Arguments:
- tokens: bfloat16 [1024, 2048], P(('group', 'inner')), may hold values from -6 to 6
- upstream: bfloat16 [1024, 2048], P(('group', 'inner')), may hold values from -6 to 6
- gate_weights: float32 [1024, 8], P(('group', 'inner')), may hold values from 0.05 to 0.5
- group_choice: int32 [1024, 4], P(('group', 'inner')), may hold values from 0 to 7, all different within a row
- pair_pick: int32 [1024, 4, 2], P(('group', 'inner')), may hold values from 0 to 15, all different within a row
- w_gate: bfloat16 [32, 4, 2048, 768], P(('group', 'inner')), may hold values from -0.125 to 0.125
- w_up: bfloat16 [32, 4, 2048, 768], P(('group', 'inner')), may hold values from -0.125 to 0.125
- w_down: bfloat16 [32, 4, 768, 2048], P(('group', 'inner')), may hold values from -0.21875 to 0.21875
Outputs:
- mixed: bfloat16 [1024, 2048], P(('group', 'inner'))
- grad_tokens: bfloat16 [1024, 2048], P(('group', 'inner'))
- grad_gate: bfloat16 [32, 4, 2048, 768], P(('group', 'inner'))
- grad_up: bfloat16 [32, 4, 2048, 768], P(('group', 'inner'))
- grad_down: bfloat16 [32, 4, 768, 2048], P(('group', 'inner'))
The draws below stay inside these ranges and needn't reach their ends.
Inputs may be any that keep to these rules, and one draw needn't show every extreme that they name: `group_choice`: each token names 4 different routing groups. `pair_pick`: the picks of one token within one routing group differ.
All inputs are finite; a program needn't handle non-finite values.
Results may differ from the reference program's by a relative error of at most 0.015.
Values may be sent and summed in bfloat16 or wider, within the bound.
No kernel may reach another device: no remote copies, remote signals or barrier semaphores. Data moves between devices by JAX's collectives and lax.ppermute only.
A program may use at most 128 MiB of HBM per device.

```python
import jax
import jax.numpy as jnp
from jax import lax

D = 2048
FF = 768
EXPERTS = 128
TOPK = 8
RGROUPS = 8
GLIMIT = 4
TOK_DEV = 32
CAP = 2
EXP_DEV = 4
SPLIT = 1
FL = 768
TOKENS = 1024
N_GROUP = 4
N_INNER = 8


def level_of(rng, extent, pieces, smallest, high):
    factor_of = 1.0
    for position, parts in pieces:
        draws = jax.random.uniform(jax.random.fold_in(jax.random.fold_in(rng, 6), position), (parts,), jnp.float32, smallest / len(pieces), high / len(pieces))
        factor_of = factor_of * jnp.repeat(jnp.exp(draws), extent[position] // parts).reshape((-1,) + (1,) * (len(extent) - 1 - position))
    return factor_of


def picks_of(own_key, rows, count, top, lift):
    sequence = jax.random.permutation(jax.random.fold_in(own_key, 1), count)
    pull = sequence
    for power in range(3):
        pull = pull * pull // count
    pull = pull * lift // count
    tickets = jax.random.randint(jax.random.fold_in(own_key, 2), (rows, count), 0, 4096) + pull
    sure = jax.random.permutation(jax.random.fold_in(own_key, 3), rows)[jnp.arange(count) % rows]
    tickets = jnp.where(jnp.arange(rows)[:, None] == sure[None, :], 1 << 14, tickets)
    score = tickets * count + jnp.arange(count)
    return lax.top_k(score.astype(jnp.int32), top)[1].astype(jnp.int32)


def normal_values(own_key, shape, width, most, cuts=(), held_as=jnp.bfloat16):
    result = width * jax.random.normal(own_key, shape, jnp.float32)
    if cuts:
        result = result * level_of(own_key, shape, cuts, -0.22, 0.18)
    return jnp.clip(result, -most, most).astype(held_as)


def setup_inputs(seed: int = 0) -> dict:
    splits = jax.random.split(jax.random.key(seed), 9)
    return {
        "tokens": normal_values(splits[0], (TOKENS, D), 1.0, 6.0, ((0, 32),)),
        "upstream": normal_values(splits[1], (TOKENS, D), 1.0, 6.0, ((0, 32),)),
        "gate_weights": jnp.clip(0.05 + 0.45 * jax.random.uniform(splits[2], (TOKENS, TOPK), jnp.float32) ** level_of(splits[2], (TOKENS, TOPK), ((0, 32),), -0.2, 0.2), 0.05, 0.5),
        "group_choice": picks_of(splits[3], TOKENS, RGROUPS, GLIMIT, 4096),
        "pair_pick": picks_of(splits[4], TOKENS * GLIMIT, EXPERTS // RGROUPS, TOPK // GLIMIT, 1024).reshape((TOKENS, GLIMIT, TOPK // GLIMIT)),
        "w_gate": normal_values(splits[5], (N_GROUP * N_INNER, EXP_DEV, D, FL), D ** -0.5, 0.125, ((0, 32),)),
        "w_up": normal_values(splits[6], (N_GROUP * N_INNER, EXP_DEV, D, FL), D ** -0.5, 0.125, ((0, 32),)),
        "w_down": normal_values(splits[7], (N_GROUP * N_INNER, EXP_DEV, FL, D), FF ** -0.5, 0.21875, ((0, 32),)),
    }


def expert_ids(group_choice, pair_pick):
    per_group = EXPERTS // RGROUPS
    joined = group_choice[:, :, None] * per_group + pair_pick
    return joined.reshape(joined.shape[0], TOPK).astype(jnp.int32)


def slot_table(ids, weights):
    flat = ids.reshape(-1)
    number = flat.shape[0]
    onehot = (flat[:, None] == jnp.arange(EXPERTS, dtype=jnp.int32)[None, :]).astype(jnp.int32)
    before = jnp.cumsum(onehot, axis=0) - onehot
    rank = jnp.sum(before * onehot, axis=1)
    target = jnp.where(rank < CAP, flat * CAP + rank, EXPERTS * CAP).astype(jnp.int32)
    owner = (jnp.arange(number, dtype=jnp.int32) // TOPK).astype(jnp.int32)
    empty = ids.shape[0]
    slot_token = jnp.full((EXPERTS * CAP + 1,), empty, jnp.int32).at[target].set(owner)[:-1]
    slot_weight = jnp.zeros((EXPERTS * CAP + 1,), jnp.float32).at[target].set(weights.reshape(-1))[:-1]
    return slot_token, slot_weight


def reference(tokens, upstream, gate_weights, group_choice, pair_pick, w_gate, w_up, w_down):
    blocks = tokens.shape[0] // TOK_DEV
    ids = expert_ids(group_choice, pair_pick).reshape(blocks, TOK_DEV, TOPK)
    slot_token, slot_weight = jax.vmap(slot_table)(ids, gate_weights.reshape(blocks, TOK_DEV, TOPK))
    offset = (jnp.arange(blocks, dtype=jnp.int32) * (TOK_DEV + 1))[:, None]
    rows = (slot_token + offset).astype(jnp.int32).reshape(blocks, EXPERTS, CAP).transpose(1, 0, 2).reshape(EXPERTS, blocks * CAP)
    scales = slot_weight.reshape(blocks, EXPERTS, CAP).transpose(1, 0, 2).reshape(EXPERTS, blocks * CAP)
    filler = jnp.zeros((blocks, 1, D), tokens.dtype)
    x_pad = jnp.concatenate([tokens.reshape(blocks, TOK_DEV, D), filler], axis=1).reshape(-1, D)
    dy_pad = jnp.concatenate([upstream.reshape(blocks, TOK_DEV, D), filler], axis=1).reshape(-1, D)
    owners = EXPERTS // EXP_DEV
    gate_all = w_gate.reshape(owners, SPLIT, EXP_DEV, D, FL)
    up_all = w_up.reshape(owners, SPLIT, EXP_DEV, D, FL)
    down_all = w_down.reshape(owners, SPLIT, EXP_DEV, FL, D)

    def step(carry, expert):
        y_acc, dx_acc = carry
        owner = expert // EXP_DEV
        within = expert % EXP_DEV
        w_g = gate_all[owner, :, within].transpose(1, 0, 2).reshape(D, FF)
        w_u = up_all[owner, :, within].transpose(1, 0, 2).reshape(D, FF)
        w_d = down_all[owner, :, within].reshape(FF, D)
        index = rows[expert]
        scale = scales[expert]
        x_rows = x_pad[index]
        dout = (scale[:, None] * dy_pad[index].astype(jnp.float32)).astype(jnp.bfloat16)
        gate = jnp.dot(x_rows, w_g, preferred_element_type=jnp.float32)
        upv = jnp.dot(x_rows, w_u, preferred_element_type=jnp.float32)
        sig = jax.nn.sigmoid(gate)
        act = gate * sig
        hidden = (act * upv).astype(jnp.bfloat16)
        out_rows = jnp.dot(hidden, w_d, preferred_element_type=jnp.float32).astype(jnp.bfloat16)
        dh = jnp.dot(dout, w_d.T, preferred_element_type=jnp.float32)
        dgate = (dh * upv * sig * (1.0 + gate * (1.0 - sig))).astype(jnp.bfloat16)
        dup = (dh * act).astype(jnp.bfloat16)
        dx_rows = (jnp.dot(dgate, w_g.T, preferred_element_type=jnp.float32)
                   + jnp.dot(dup, w_u.T, preferred_element_type=jnp.float32)).astype(jnp.bfloat16)
        g_gate = jnp.dot(x_rows.T, dgate, preferred_element_type=jnp.float32).astype(jnp.bfloat16)
        g_up = jnp.dot(x_rows.T, dup, preferred_element_type=jnp.float32).astype(jnp.bfloat16)
        g_down = jnp.dot(hidden.T, dout, preferred_element_type=jnp.float32).astype(jnp.bfloat16)
        y_acc = y_acc.at[index].add(scale[:, None] * out_rows.astype(jnp.float32))
        dx_acc = dx_acc.at[index].add(dx_rows.astype(jnp.float32))
        return (y_acc, dx_acc), (g_gate, g_up, g_down)

    start = (jnp.zeros((x_pad.shape[0], D), jnp.float32), jnp.zeros((x_pad.shape[0], D), jnp.float32))
    (y_acc, dx_acc), (g_gate, g_up, g_down) = lax.scan(step, start, jnp.arange(EXPERTS, dtype=jnp.int32))
    mixed = y_acc.reshape(blocks, TOK_DEV + 1, D)[:, :TOK_DEV].reshape(-1, D).astype(jnp.bfloat16)
    grad_tokens = dx_acc.reshape(blocks, TOK_DEV + 1, D)[:, :TOK_DEV].reshape(-1, D).astype(jnp.bfloat16)
    grad_gate = g_gate.reshape(owners, EXP_DEV, D, SPLIT, FL).transpose(0, 3, 1, 2, 4).reshape(owners * SPLIT, EXP_DEV, D, FL)
    grad_up = g_up.reshape(owners, EXP_DEV, D, SPLIT, FL).transpose(0, 3, 1, 2, 4).reshape(owners * SPLIT, EXP_DEV, D, FL)
    grad_down = g_down.reshape(owners, EXP_DEV, SPLIT, FL, D).transpose(0, 2, 1, 3, 4).reshape(owners * SPLIT, EXP_DEV, FL, D)
    return (mixed, grad_tokens, grad_gate, grad_up, grad_down)
```

```python
import functools

import jax
import jax.numpy as jnp
from jax import lax
from jax.experimental import pallas as pl
from jax.experimental.pallas import tpu as pltpu
from jax.sharding import PartitionSpec as P


EXPERTS = 128
TOPK = 8
RGROUPS = 8
CAP = 2


def expert_ids(group_choice, pair_pick):
    per_group = EXPERTS // RGROUPS
    joined = group_choice[:, :, None] * per_group + pair_pick
    return joined.reshape(joined.shape[0], TOPK)


def slot_table(ids, weights):
    flat = ids.reshape(-1)
    number = flat.shape[0]
    onehot = (flat[:, None] == jnp.arange(EXPERTS, dtype=jnp.int32)[None, :]).astype(jnp.int32)
    before = jnp.cumsum(onehot, axis=0) - onehot
    rank = jnp.sum(before * onehot, axis=1)
    target = jnp.where(rank < CAP, flat * CAP + rank, EXPERTS * CAP)
    owner = jnp.arange(number, dtype=jnp.int32) // TOPK
    empty = ids.shape[0]
    slot_token = jnp.full((EXPERTS * CAP + 1,), empty, jnp.int32).at[target].set(owner)[:-1]
    slot_weight = (
        jnp.zeros((EXPERTS * CAP + 1,), jnp.float32).at[target].set(weights.reshape(-1))[:-1]
    )
    return (slot_token, slot_weight)


def dispatch(rows, groups, inner, split, slots, width):
    local, owners, joined = rows.shape
    copies = jnp.broadcast_to(rows[:, :, None], (local, owners, split, joined))
    copies = copies.reshape(local, groups, inner, joined)
    received = lax.all_to_all(
        lax.all_to_all(copies, "group", split_axis=1, concat_axis=1, tiled=True),
        "inner",
        split_axis=2,
        concat_axis=2,
        tiled=True,
    )
    return received.reshape(local, groups * inner * slots, width)


def send_back(partial_value, groups, inner, split):
    local, total, width = partial_value.shape
    slots = total // (groups * inner)
    owners = groups * inner // split
    returned = lax.all_to_all(
        lax.all_to_all(
            partial_value.reshape(local, groups, inner, slots * width).astype(jnp.bfloat16),
            "group",
            split_axis=1,
            concat_axis=1,
            tiled=True,
        ),
        "inner",
        split_axis=2,
        concat_axis=2,
        tiled=True,
    ).astype(jnp.float32)
    returned = jnp.sum(returned.reshape(local, owners, split, slots * width), axis=2).astype(
        jnp.bfloat16
    )
    return returned.reshape(local * owners * slots, width)


def on_device_general(tokens, upstream, gate_weights, group_choice, pair_pick, w_gate, w_up, w_down):
    groups = lax.axis_size("group")
    inner = lax.axis_size("inner")
    devices = groups * inner
    local = w_gate.shape[1]
    split = devices * local // EXPERTS
    owners = devices // split
    count = tokens.shape[0]
    width = tokens.shape[1]
    ids = expert_ids(group_choice, pair_pick)
    slot_token, slot_weight = slot_table(ids, gate_weights)
    order_token = slot_token.reshape(owners, local, CAP).transpose(1, 0, 2).reshape(-1)
    order_weight = slot_weight.reshape(owners, local, CAP).transpose(1, 0, 2).reshape(-1)
    filler = jnp.zeros((1, width), tokens.dtype)
    x_pad = jnp.concatenate([tokens, filler], axis=0)
    dy_pad = jnp.concatenate([upstream, filler], axis=0)
    x_rows = x_pad[order_token].reshape(local, owners, CAP * width)
    x_recv = dispatch(x_rows, groups, inner, split, CAP, width)
    w_g = w_gate[0]
    w_u = w_up[0]
    w_d = w_down[0]
    gate = jnp.einsum("lrd,ldf->lrf", x_recv, w_g, preferred_element_type=jnp.float32)
    upv = jnp.einsum("lrd,ldf->lrf", x_recv, w_u, preferred_element_type=jnp.float32)
    sig = jax.nn.sigmoid(gate)
    act = gate * sig
    hidden = (act * upv).astype(jnp.bfloat16)
    out_partial = jnp.einsum("lrf,lfd->lrd", hidden, w_d, preferred_element_type=jnp.float32)
    out_values = send_back(out_partial, groups, inner, split)
    onehot = order_token[None, :] == jnp.arange(count, dtype=jnp.int32)[:, None]
    blend = jnp.where(onehot, order_weight[None, :], 0.0)
    mixed = jnp.dot(
        blend,
        out_values.astype(jnp.float32),
        precision=lax.Precision.HIGHEST,
        preferred_element_type=jnp.float32,
    ).astype(jnp.bfloat16)
    dout_rows = (order_weight[:, None] * dy_pad[order_token].astype(jnp.float32)).astype(
        jnp.bfloat16
    )
    dout = dispatch(dout_rows.reshape(local, owners, CAP * width), groups, inner, split, CAP, width)
    dh = jnp.einsum("lrd,lfd->lrf", dout, w_d, preferred_element_type=jnp.float32)
    dgate = (dh * upv * sig * (1.0 + gate * (1.0 - sig))).astype(jnp.bfloat16)
    dup = (dh * act).astype(jnp.bfloat16)
    dx_partial = jnp.einsum(
        "lrf,ldf->lrd", dgate, w_g, preferred_element_type=jnp.float32
    ) + jnp.einsum("lrf,ldf->lrd", dup, w_u, preferred_element_type=jnp.float32)
    grad_gate = jnp.einsum(
        "lrd,lrf->ldf", x_recv, dgate, preferred_element_type=jnp.float32
    ).astype(jnp.bfloat16)
    grad_up = jnp.einsum("lrd,lrf->ldf", x_recv, dup, preferred_element_type=jnp.float32).astype(
        jnp.bfloat16
    )
    grad_down = jnp.einsum("lrf,lrd->lfd", hidden, dout, preferred_element_type=jnp.float32).astype(
        jnp.bfloat16
    )
    dx_values = send_back(dx_partial, groups, inner, split)
    select = onehot.astype(jnp.bfloat16)
    grad_tokens = jnp.dot(select, dx_values, preferred_element_type=jnp.float32).astype(
        jnp.bfloat16
    )
    return (mixed, grad_tokens, grad_gate[None], grad_up[None], grad_down[None])


COLUMNS = 4
PLACES = 8
TABLE = 128
MIB = 1024 * 1024


def params(mib, rank=0):
    return pltpu.CompilerParams(
        vmem_limit_bytes=mib * MIB,
        dimension_semantics=("arbitrary",) * rank if rank else None,
    )


def cost(flops, moved):
    return pl.CostEstimate(flops=int(flops), bytes_accessed=int(moved), transcendentals=0)


def swap(value, axis, size, mask):
    return lax.ppermute(value, axis, [(k, k ^ mask) for k in range(size)])


def whole():
    return pl.BlockSpec(memory_space=pltpu.VMEM)


def select_tokens_kernel(local, count, width, place_ref, *refs):
    pieces, rest = refs[:PLACES], refs[PLACES:]
    near, rest = rest[: PLACES // 2], rest[PLACES // 2 :]
    far, rest = rest[0], rest[1:]
    outs, (pick_ref, pick_t_ref, high_ref, low_ref, scale_ref), full = rest[:COLUMNS], rest[COLUMNS:-1], rest[-1]
    total = PLACES * count
    rows = COLUMNS * local * PLACES * CAP
    tables = []
    for j in range(PLACES):
        full[j * count : (j + 1) * count, :] = pieces[j][...]
        tables.append(far[j // 2] if j % 2 else near[j // 2][...])
    table = jnp.concatenate(tables, axis=0)
    row = lax.broadcasted_iota(jnp.int32, (1, rows), 1)
    slot = row % CAP
    piece = row // CAP % PLACES
    column = place_ref[0] ^ (row // (CAP * PLACES * local))
    expert = (column * PLACES + place_ref[1]) * local + row // (CAP * PLACES) % local
    expert = expert.astype(jnp.float32)
    member = jnp.zeros((total, rows), jnp.float32)
    weight = jnp.zeros((total, rows), jnp.float32)
    for k in range(TOPK):
        same = table[:, k : k + 1] == expert
        value = table[:, TOPK + k : TOPK + k + 1]
        member = jnp.where(same, 1.0, member)
        weight = jnp.where(same, value, weight)
    token = lax.broadcasted_iota(jnp.int32, (total, 1), 0)
    other = lax.broadcasted_iota(jnp.int32, (1, total), 1)
    earlier = ((other < token) & (other // count == token // count)).astype(jnp.float32)
    rank = jnp.dot(
        earlier.astype(jnp.bfloat16), member.astype(jnp.bfloat16), preferred_element_type=jnp.float32
    )
    kept = (member > 0.5) & (rank == slot.astype(jnp.float32)) & (token // count == piece)
    pick_t = jnp.where(kept, 1.0, 0.0)
    weight = jnp.where(kept, weight, 0.0)
    high = weight.astype(jnp.bfloat16)
    pick = pick_t.T.astype(jnp.bfloat16)
    pick_ref[...] = pick
    pick_t_ref[...] = pick_t.astype(jnp.bfloat16)
    high_ref[...] = high
    low_ref[...] = (weight - high.astype(jnp.float32)).astype(jnp.bfloat16)
    scale_ref[...] = jnp.sum(weight.T, axis=1, keepdims=True)
    chosen = jnp.dot(pick, full[...], preferred_element_type=jnp.float32).astype(jnp.bfloat16)
    part = rows // COLUMNS
    for m in range(COLUMNS):
        outs[m][...] = chosen[m * part : (m + 1) * part].reshape(outs[m].shape)


def select_upstream_kernel(count, pick_ref, scale_ref, *refs):
    pieces, outs, full = refs[:PLACES], refs[PLACES:-1], refs[-1]
    for j in range(PLACES):
        full[j * count : (j + 1) * count, :] = pieces[j][...]
    chosen = jnp.dot(pick_ref[...], full[...], preferred_element_type=jnp.float32)
    chosen = (chosen * scale_ref[...]).astype(jnp.bfloat16)
    part = chosen.shape[0] // COLUMNS
    for m in range(COLUMNS):
        outs[m][...] = chosen[m * part : (m + 1) * part].reshape(outs[m].shape)


def combine_kernel(count, terms, *refs):
    blends, pieces, (even_ref, odd_ref, full) = refs[:terms], refs[terms : terms + COLUMNS], refs[terms + COLUMNS :]
    width = full.shape[1]
    part = full.shape[0] // COLUMNS
    for m in range(COLUMNS):
        full[m * part : (m + 1) * part, :] = pieces[m][...].reshape(part, width)
    value = jnp.dot(blends[0][...], full[...], preferred_element_type=jnp.float32)
    for blend in blends[1:]:
        value = value + jnp.dot(blend[...], full[...], preferred_element_type=jnp.float32)
    value = value.astype(jnp.bfloat16)
    for j in range(PLACES):
        target = odd_ref if j % 2 else even_ref
        target[j // 2] = value[j * count : (j + 1) * count]


def across(a, b):
    return lax.dot_general(a, b, (((1,), (1,)), ((), ())), preferred_element_type=jnp.float32)


def down(a, b):
    return lax.dot_general(a, b, (((0,), (0,)), ((), ())), preferred_element_type=jnp.float32)


def joined(pieces, e):
    return jnp.concatenate([piece[e] for piece in pieces], axis=0)


def forward_kernel(*refs):
    pieces = refs[:COLUMNS]
    wg_ref, wu_ref, wd_ref, g_ref, u_ref, h_ref = refs[COLUMNS : COLUMNS + 6]
    outs = refs[COLUMNS + 6 :]
    part = outs[0].shape[1]

    @pl.loop(0, wg_ref.shape[1])
    def _(e):
        rows = joined(pieces, e)
        g = jnp.dot(rows, wg_ref[0, e], preferred_element_type=jnp.float32)
        u = jnp.dot(rows, wu_ref[0, e], preferred_element_type=jnp.float32)
        h = (g * jax.nn.sigmoid(g) * u).astype(jnp.bfloat16)
        g_ref[e] = g
        u_ref[e] = u
        h_ref[e] = h
        value = jnp.dot(h, wd_ref[0, e], preferred_element_type=jnp.float32).astype(jnp.bfloat16)
        for m in range(COLUMNS):
            outs[m][e] = value[m * part : (m + 1) * part]


def backward_kernel(*refs):
    pieces = refs[:COLUMNS]
    g_ref, u_ref, wg_ref, wu_ref, wd_ref, dg_ref, du_ref = refs[COLUMNS : COLUMNS + 7]
    outs = refs[COLUMNS + 7 :]
    part = outs[0].shape[1]

    @pl.loop(0, wg_ref.shape[1])
    def _(e):
        dh = across(joined(pieces, e), wd_ref[0, e])
        g = g_ref[e]
        sig = jax.nn.sigmoid(g)
        dg = (dh * u_ref[e] * sig * (1.0 + g * (1.0 - sig))).astype(jnp.bfloat16)
        du = (dh * (g * sig)).astype(jnp.bfloat16)
        dg_ref[e] = dg
        du_ref[e] = du
        value = (across(dg, wg_ref[0, e]) + across(du, wu_ref[0, e])).astype(jnp.bfloat16)
        for m in range(COLUMNS):
            outs[m][e] = value[m * part : (m + 1) * part]


def up_grads_kernel(*refs):
    pieces = refs[:COLUMNS]
    dg_ref, du_ref, gg_ref, gu_ref = refs[COLUMNS:]
    rows = joined(pieces, 0)
    gg_ref[0, 0] = down(rows, dg_ref[0]).astype(jnp.bfloat16)
    gu_ref[0, 0] = down(rows, du_ref[0]).astype(jnp.bfloat16)


def down_grads_kernel(*refs):
    pieces = refs[:COLUMNS]
    h_ref, gd_ref = refs[COLUMNS:]
    gd_ref[0, 0] = down(h_ref[0], joined(pieces, 0)).astype(jnp.bfloat16)


def after(value, *others):
    return lax.optimization_barrier((value, *others))[0]


def on_device(tokens, upstream, gate_weights, group_choice, pair_pick, w_gate, w_up, w_down):
    count, width = tokens.shape
    local, hidden = w_gate.shape[1], w_gate.shape[3]
    rows = COLUMNS * local * PLACES * CAP
    part = PLACES * CAP
    bf16, f32 = jnp.bfloat16, jnp.float32

    def along(value):
        return [value] + [swap(value, "inner", PLACES, 2 * z) for z in (1, 2, 3)]

    def both(near):
        return [one for z in near for one in (z, swap(z, "inner", PLACES, 1))]

    def exchange(pieces):
        return [pieces[0]] + [swap(pieces[m], "group", COLUMNS, m) for m in (1, 2, 3)]

    ids = expert_ids(group_choice, pair_pick)
    blank = jnp.zeros((count, TABLE - 2 * TOPK), f32)
    table = jnp.concatenate([ids.astype(f32), gate_weights, blank], axis=1)
    x_near = along(tokens)
    table_near = along(table)
    table_far = swap(jnp.stack(table_near), "inner", PLACES, 1)

    sent = [jax.ShapeDtypeStruct((local, part, width), bf16)] * COLUMNS
    square = jax.ShapeDtypeStruct((rows, rows), bf16)
    place = jnp.stack([lax.axis_index("group"), lax.axis_index("inner")]).astype(jnp.int32)
    *x_send, pick, pick_t, high, low, scale = pl.pallas_call(
        functools.partial(select_tokens_kernel, local, count, width),
        name="select_tokens",
        out_shape=sent + [square] * 4 + [jax.ShapeDtypeStruct((rows, 1), f32)],
        in_specs=[pl.BlockSpec(memory_space=pltpu.SMEM)] + [whole()] * (PLACES + PLACES // 2 + 1),
        out_specs=[whole()] * (COLUMNS + 5),
        scratch_shapes=[pltpu.VMEM((PLACES * count, width), bf16)],
        compiler_params=params(8),
        cost_estimate=cost(2 * rows * rows * width, 4 * rows * width),
    )(place, *both(x_near), *table_near, table_far)
    x_recv = exchange(x_send)

    dy_near = along(after(upstream, *x_near[1:]))
    dy_send = pl.pallas_call(
        functools.partial(select_upstream_kernel, count),
        name="select_upstream",
        out_shape=sent,
        in_specs=[whole()] * (PLACES + 2),
        out_specs=[whole()] * COLUMNS,
        scratch_shapes=[pltpu.VMEM((PLACES * count, width), bf16)],
        compiler_params=params(8),
        cost_estimate=cost(2 * rows * rows * width, 4 * rows * width),
    )(pick, scale, *both(dy_near))
    dy_recv = exchange(dy_send)

    hid = lambda t: jax.ShapeDtypeStruct((local, rows // local, hidden), t)
    weight_bytes = 2 * local * width * hidden
    flops = 2 * rows * width * hidden

    g, u, h, *out_send = pl.pallas_call(
        forward_kernel,
        name="forward",
        out_shape=[hid(f32), hid(f32), hid(bf16)] + sent,
        in_specs=[whole()] * (COLUMNS + 3),
        out_specs=[whole()] * (COLUMNS + 3),
        compiler_params=params(8),
        cost_estimate=cost(12 * flops, 3 * weight_bytes),
    )(after(x_recv[0], *dy_send), *x_recv[1:], w_gate, w_up, w_down)
    out_back = exchange(out_send)

    dg, du, *dx_send = pl.pallas_call(
        backward_kernel,
        name="backward",
        out_shape=[hid(bf16), hid(bf16)] + sent,
        in_specs=[whole()] * (COLUMNS + 5),
        out_specs=[whole()] * (COLUMNS + 2),
        compiler_params=params(8),
        cost_estimate=cost(12 * flops, 3 * weight_bytes),
    )(*dy_recv, g, u, w_gate, w_up, w_down)
    dx_back = exchange(dx_send)

    def combine(blends, pieces, name):
        half = jax.ShapeDtypeStruct((PLACES // 2, count, width), bf16)
        even, odd = pl.pallas_call(
            functools.partial(combine_kernel, count, len(blends)),
            name=name,
            out_shape=[half, half],
            in_specs=[whole()] * (len(blends) + COLUMNS),
            out_specs=[whole()] * 2,
            scratch_shapes=[pltpu.VMEM((rows, width), bf16)],
            compiler_params=params(8),
            cost_estimate=cost(2 * rows * rows * width, 4 * rows * width),
        )(*blends, *pieces)
        other = swap(odd, "inner", PLACES, 1)
        sums = [even[z].astype(f32) + other[z].astype(f32) for z in range(PLACES // 2)]
        return sums[0], [sums[z].astype(bf16) for z in (1, 2, 3)]

    def finish(total, parts):
        for z in (1, 2, 3):
            total = total + swap(parts[z - 1], "inner", PLACES, 2 * z).astype(f32)
        return total.astype(bf16)

    slot_spec = pl.BlockSpec((1, part, width), lambda e: (e, 0, 0))
    hid_spec = pl.BlockSpec((1, rows // local, hidden), lambda e: (e, 0, 0))
    up_spec = pl.BlockSpec((1, 1, width, hidden), lambda e: (0, e, 0, 0))
    down_spec = pl.BlockSpec((1, 1, hidden, width), lambda e: (0, e, 0, 0))

    out_own, out_parts = combine([high, low], [after(out_back[0], *dx_send)] + out_back[1:], "combine_out")
    mixed = finish(out_own, out_parts)
    grad_down = pl.pallas_call(
        down_grads_kernel,
        name="down_grads",
        grid=(local,),
        out_shape=jax.ShapeDtypeStruct(w_down.shape, bf16),
        in_specs=[slot_spec] * COLUMNS + [hid_spec],
        out_specs=down_spec,
        compiler_params=params(32, 1),
        cost_estimate=cost(4 * flops, weight_bytes),
    )(*dy_recv, after(h, *out_parts))

    dx_own, dx_parts = combine([pick_t], [after(dx_back[0], grad_down)] + dx_back[1:], "combine_dx")
    grad_tokens = finish(dx_own, dx_parts)
    grad_gate, grad_up = pl.pallas_call(
        up_grads_kernel,
        name="up_grads",
        grid=(local,),
        out_shape=[jax.ShapeDtypeStruct(w.shape, bf16) for w in (w_gate, w_up)],
        in_specs=[slot_spec] * COLUMNS + [hid_spec] * 2,
        out_specs=[up_spec, up_spec],
        compiler_params=params(32, 1),
        cost_estimate=cost(8 * flops, 2 * weight_bytes),
    )(*x_recv, after(dg, *dx_parts), du)
    return (mixed, grad_tokens, grad_gate, grad_up, grad_down)


def solution(mesh):
    ours = mesh.shape["group"] == COLUMNS and mesh.shape["inner"] == PLACES
    in_specs = (
        P(("group", "inner"), None),
        P(("group", "inner"), None),
        P(("group", "inner"), None),
        P(("group", "inner"), None),
        P(("group", "inner"), None, None),
        P(("group", "inner"), None, None, None),
        P(("group", "inner"), None, None, None),
        P(("group", "inner"), None, None, None),
    )
    out_specs = (
        P(("group", "inner"), None),
        P(("group", "inner"), None),
        P(("group", "inner"), None, None, None),
        P(("group", "inner"), None, None, None),
        P(("group", "inner"), None, None, None),
    )
    return jax.shard_map(
        on_device if ours else on_device_general, mesh=mesh, in_specs=in_specs, out_specs=out_specs, check_vma=False
    )
```

```python
import functools

import jax
import jax.numpy as jnp
from jax import lax
from jax.experimental import pallas as pl
from jax.experimental.pallas import tpu as pltpu
from jax.sharding import PartitionSpec as P


EXPERTS = 128
TOPK = 8
RGROUPS = 8
GLIMIT = 4
CAP = 2


def expert_ids(group_choice, pair_pick):
    per_group = EXPERTS // RGROUPS
    joined = group_choice[:, :, None] * per_group + pair_pick
    return joined.reshape(joined.shape[0], TOPK)


def slot_table(ids, weights):
    flat = ids.reshape(-1)
    number = flat.shape[0]
    onehot = (flat[:, None] == jnp.arange(EXPERTS, dtype=jnp.int32)[None, :]).astype(jnp.int32)
    before = jnp.cumsum(onehot, axis=0) - onehot
    rank = jnp.sum(before * onehot, axis=1)
    target = jnp.where(rank < CAP, flat * CAP + rank, EXPERTS * CAP)
    owner = jnp.arange(number, dtype=jnp.int32) // TOPK
    empty = ids.shape[0]
    slot_token = jnp.full((EXPERTS * CAP + 1,), empty, jnp.int32).at[target].set(owner)[:-1]
    slot_weight = (
        jnp.zeros((EXPERTS * CAP + 1,), jnp.float32).at[target].set(weights.reshape(-1))[:-1]
    )
    return (slot_token, slot_weight)


def dispatch(rows, groups, inner, split, slots, width):
    local, owners, joined = rows.shape
    copies = jnp.broadcast_to(rows[:, :, None], (local, owners, split, joined))
    copies = copies.reshape(local, groups, inner, joined)
    received = lax.all_to_all(
        lax.all_to_all(copies, "group", split_axis=1, concat_axis=1, tiled=True),
        "inner",
        split_axis=2,
        concat_axis=2,
        tiled=True,
    )
    return received.reshape(local, groups * inner * slots, width)


def send_back(partial_value, groups, inner, split):
    local, total, width = partial_value.shape
    slots = total // (groups * inner)
    owners = groups * inner // split
    returned = lax.all_to_all(
        lax.all_to_all(
            partial_value.reshape(local, groups, inner, slots * width).astype(jnp.bfloat16),
            "group",
            split_axis=1,
            concat_axis=1,
            tiled=True,
        ),
        "inner",
        split_axis=2,
        concat_axis=2,
        tiled=True,
    ).astype(jnp.float32)
    returned = jnp.sum(returned.reshape(local, owners, split, slots * width), axis=2).astype(
        jnp.bfloat16
    )
    return returned.reshape(local * owners * slots, width)


def on_device_general(tokens, upstream, gate_weights, group_choice, pair_pick, w_gate, w_up, w_down):
    groups = lax.axis_size("group")
    inner = lax.axis_size("inner")
    devices = groups * inner
    local = w_gate.shape[1]
    split = devices * local // EXPERTS
    owners = devices // split
    count = tokens.shape[0]
    width = tokens.shape[1]
    ids = expert_ids(group_choice, pair_pick)
    slot_token, slot_weight = slot_table(ids, gate_weights)
    order_token = slot_token.reshape(owners, local, CAP).transpose(1, 0, 2).reshape(-1)
    order_weight = slot_weight.reshape(owners, local, CAP).transpose(1, 0, 2).reshape(-1)
    filler = jnp.zeros((1, width), tokens.dtype)
    x_pad = jnp.concatenate([tokens, filler], axis=0)
    dy_pad = jnp.concatenate([upstream, filler], axis=0)
    x_rows = x_pad[order_token].reshape(local, owners, CAP * width)
    x_recv = dispatch(x_rows, groups, inner, split, CAP, width)
    w_g = w_gate[0]
    w_u = w_up[0]
    w_d = w_down[0]
    gate = jnp.einsum("lrd,ldf->lrf", x_recv, w_g, preferred_element_type=jnp.float32)
    upv = jnp.einsum("lrd,ldf->lrf", x_recv, w_u, preferred_element_type=jnp.float32)
    sig = jax.nn.sigmoid(gate)
    act = gate * sig
    hidden = (act * upv).astype(jnp.bfloat16)
    out_partial = jnp.einsum("lrf,lfd->lrd", hidden, w_d, preferred_element_type=jnp.float32)
    out_values = send_back(out_partial, groups, inner, split)
    onehot = order_token[None, :] == jnp.arange(count, dtype=jnp.int32)[:, None]
    blend = jnp.where(onehot, order_weight[None, :], 0.0)
    mixed = jnp.dot(
        blend,
        out_values.astype(jnp.float32),
        precision=lax.Precision.HIGHEST,
        preferred_element_type=jnp.float32,
    ).astype(jnp.bfloat16)
    dout_rows = (order_weight[:, None] * dy_pad[order_token].astype(jnp.float32)).astype(
        jnp.bfloat16
    )
    dout = dispatch(dout_rows.reshape(local, owners, CAP * width), groups, inner, split, CAP, width)
    dh = jnp.einsum("lrd,lfd->lrf", dout, w_d, preferred_element_type=jnp.float32)
    dgate = (dh * upv * sig * (1.0 + gate * (1.0 - sig))).astype(jnp.bfloat16)
    dup = (dh * act).astype(jnp.bfloat16)
    dx_partial = jnp.einsum(
        "lrf,ldf->lrd", dgate, w_g, preferred_element_type=jnp.float32
    ) + jnp.einsum("lrf,ldf->lrd", dup, w_u, preferred_element_type=jnp.float32)
    grad_gate = jnp.einsum(
        "lrd,lrf->ldf", x_recv, dgate, preferred_element_type=jnp.float32
    ).astype(jnp.bfloat16)
    grad_up = jnp.einsum("lrd,lrf->ldf", x_recv, dup, preferred_element_type=jnp.float32).astype(
        jnp.bfloat16
    )
    grad_down = jnp.einsum("lrf,lrd->lfd", hidden, dout, preferred_element_type=jnp.float32).astype(
        jnp.bfloat16
    )
    dx_values = send_back(dx_partial, groups, inner, split)
    select = onehot.astype(jnp.bfloat16)
    grad_tokens = jnp.dot(select, dx_values, preferred_element_type=jnp.float32).astype(
        jnp.bfloat16
    )
    return (mixed, grad_tokens, grad_gate[None], grad_up[None], grad_down[None])


COLUMNS = 4
PLACES = 8
TABLE = 128
MIB = 1024 * 1024


def params(mib, rank=0):
    return pltpu.CompilerParams(
        vmem_limit_bytes=mib * MIB,
        dimension_semantics=("arbitrary",) * rank if rank else None,
    )


def cost(flops, moved):
    return pl.CostEstimate(flops=int(flops), bytes_accessed=int(moved), transcendentals=0)


def swap(value, axis, size, mask):
    return lax.ppermute(value, axis, [(k, k ^ mask) for k in range(size)])


def whole():
    return pl.BlockSpec(memory_space=pltpu.VMEM)


def pack_kernel(tokens_ref, upstream_ref, choice_ref, pick_ref, weight_ref, packed_ref):
    count, width = tokens_ref.shape
    per_group = EXPERTS // RGROUPS
    parts = []
    for k in range(TOPK):
        group, place = choice_ref[k // 2 : k // 2 + 1, :], pick_ref[k // 2, k % 2 : k % 2 + 1, :]
        parts.append((group * per_group + place).astype(jnp.float32))
    left = weight_ref[...]
    for _ in range(3):
        high = left.astype(jnp.bfloat16).astype(jnp.float32)
        parts.append(high)
        left = left - high
    parts.append(jnp.zeros((TABLE - 4 * TOPK, count), jnp.float32))
    packed_ref[:, :width] = tokens_ref[...]
    packed_ref[:, width : 2 * width] = upstream_ref[...]
    packed_ref[:, 2 * width :] = jnp.concatenate(parts, axis=0).T.astype(jnp.bfloat16)


def select_kernel(local, count, place_ref, *refs):
    pieces, rest = refs[:PLACES], refs[PLACES:]
    x_outs, dy_outs, rest = rest[:COLUMNS], rest[COLUMNS : 2 * COLUMNS], rest[2 * COLUMNS :]
    pick_t_ref, high_ref, low_ref, full = rest
    width = full.shape[1] // 2
    total = PLACES * count
    rows = COLUMNS * local * PLACES * CAP
    for j in range(PLACES):
        full[j * count : (j + 1) * count, :] = pieces[j][:, : full.shape[1]]
    table = jnp.concatenate([piece[:, full.shape[1] :].astype(jnp.float32) for piece in pieces], axis=0).T
    row = lax.broadcasted_iota(jnp.int32, (rows, 1), 0)
    slot = row % CAP
    piece = row // CAP % PLACES
    column = place_ref[0] ^ (row // (CAP * PLACES * local))
    expert = (column * PLACES + place_ref[1]) * local + row // (CAP * PLACES) % local
    expert = expert.astype(jnp.float32)
    member = jnp.zeros((rows, total), jnp.float32)
    weight = jnp.zeros((rows, total), jnp.float32)
    for k in range(TOPK):
        same = table[k : k + 1, :] == expert
        member = jnp.where(same, 1.0, member)
        value = table[TOPK + k : TOPK + k + 1, :] + table[2 * TOPK + k : 2 * TOPK + k + 1, :]
        value = value + table[3 * TOPK + k : 3 * TOPK + k + 1, :]
        weight = jnp.where(same, value, weight)
    other = lax.broadcasted_iota(jnp.int32, (total, 1), 0)
    token = lax.broadcasted_iota(jnp.int32, (1, total), 1)
    earlier = ((other < token) & (other // count == token // count)).astype(jnp.float32)
    rank = jnp.dot(
        member.astype(jnp.bfloat16), earlier.astype(jnp.bfloat16), preferred_element_type=jnp.float32
    )
    kept = (member > 0.5) & (rank == slot.astype(jnp.float32)) & (token // count == piece)
    pick = jnp.where(kept, 1.0, 0.0)
    weight = jnp.where(kept, weight, 0.0)
    scale = jnp.sum(weight, axis=1, keepdims=True)
    chosen = jnp.dot(pick.astype(jnp.bfloat16), full[...], preferred_element_type=jnp.float32)
    x_rows = chosen[:, :width].astype(jnp.bfloat16)
    dy_rows = (chosen[:, width:] * scale).astype(jnp.bfloat16)
    part = rows // COLUMNS
    for m in range(COLUMNS):
        x_outs[m][...] = x_rows[m * part : (m + 1) * part].reshape(x_outs[m].shape)
        dy_outs[m][...] = dy_rows[m * part : (m + 1) * part].reshape(dy_outs[m].shape)
    pick_t_ref[...] = pick.T.astype(jnp.bfloat16)
    weight = weight.T
    high = weight.astype(jnp.bfloat16)
    high_ref[...] = high
    low_ref[...] = (weight - high.astype(jnp.float32)).astype(jnp.bfloat16)


def combine_kernel(count, terms, *refs):
    blends, pieces, (even_ref, odd_ref, full) = refs[:terms], refs[terms : terms + COLUMNS], refs[terms + COLUMNS :]
    width = full.shape[1]
    part = full.shape[0] // COLUMNS
    for m in range(COLUMNS):
        full[m * part : (m + 1) * part, :] = pieces[m][...].reshape(part, width)
    value = jnp.dot(blends[0][...], full[...], preferred_element_type=jnp.float32)
    for blend in blends[1:]:
        value = value + jnp.dot(blend[...], full[...], preferred_element_type=jnp.float32)
    value = value.astype(jnp.bfloat16)
    for j in range(PLACES):
        target = odd_ref if j % 2 else even_ref
        target[j // 2] = value[j * count : (j + 1) * count]


def across(a, b):
    return lax.dot_general(a, b, (((1,), (1,)), ((), ())), preferred_element_type=jnp.float32)


def down(a, b):
    return lax.dot_general(a, b, (((0,), (0,)), ((), ())), preferred_element_type=jnp.float32)


def joined(pieces, e):
    return jnp.concatenate([piece[e] for piece in pieces], axis=0)


def load_kernel(source_ref, held_ref, done):
    copy = pltpu.make_async_copy(source_ref, held_ref, done)
    copy.start()
    copy.wait()


def forward_kernel(*refs):
    pieces = refs[:COLUMNS]
    wg_ref, wu_ref, wd_ref, g_ref, u_ref, h_ref = refs[COLUMNS : COLUMNS + 6]
    outs = refs[COLUMNS + 6 :]
    part = outs[0].shape[1]

    @pl.loop(0, wg_ref.shape[1])
    def _(e):
        rows = joined(pieces, e)
        g = jnp.dot(rows, wg_ref[0, e], preferred_element_type=jnp.float32)
        u = jnp.dot(rows, wu_ref[0, e], preferred_element_type=jnp.float32)
        h = (g * jax.nn.sigmoid(g) * u).astype(jnp.bfloat16)
        g_ref[e] = g
        u_ref[e] = u
        h_ref[e] = h
        value = jnp.dot(h, wd_ref[0, e], preferred_element_type=jnp.float32).astype(jnp.bfloat16)
        for m in range(COLUMNS):
            outs[m][e] = value[m * part : (m + 1) * part]


def backward_kernel(*refs):
    pieces = refs[:COLUMNS]
    g_ref, u_ref, wg_ref, wu_ref, wd_ref, dg_ref, du_ref = refs[COLUMNS : COLUMNS + 7]
    outs = refs[COLUMNS + 7 :]
    part = outs[0].shape[1]

    @pl.loop(0, wg_ref.shape[1])
    def _(e):
        dh = across(joined(pieces, e), wd_ref[0, e])
        g = g_ref[e]
        sig = jax.nn.sigmoid(g)
        dg = (dh * u_ref[e] * sig * (1.0 + g * (1.0 - sig))).astype(jnp.bfloat16)
        du = (dh * (g * sig)).astype(jnp.bfloat16)
        dg_ref[e] = dg
        du_ref[e] = du
        value = (across(dg, wg_ref[0, e]) + across(du, wu_ref[0, e])).astype(jnp.bfloat16)
        for m in range(COLUMNS):
            outs[m][e] = value[m * part : (m + 1) * part]


def up_grads_kernel(*refs):
    pieces = refs[:COLUMNS]
    dg_ref, du_ref, gg_ref, gu_ref = refs[COLUMNS:]
    rows = joined(pieces, 0)
    gg_ref[0, 0] = down(rows, dg_ref[0]).astype(jnp.bfloat16)
    gu_ref[0, 0] = down(rows, du_ref[0]).astype(jnp.bfloat16)


def down_grads_kernel(*refs):
    pieces = refs[:COLUMNS]
    h_ref, gd_ref = refs[COLUMNS:]
    gd_ref[0, 0] = down(h_ref[0], joined(pieces, 0)).astype(jnp.bfloat16)


def after(value, *others):
    return lax.optimization_barrier((value, *others))[0]


def on_device(tokens, upstream, gate_weights, group_choice, pair_pick, w_gate, w_up, w_down):
    count, width = tokens.shape
    local, hidden = w_gate.shape[1], w_gate.shape[3]
    if COLUMNS * PLACES * local != EXPERTS or local * PLACES * CAP != 2 * count:
        return on_device_general(
            tokens, upstream, gate_weights, group_choice, pair_pick, w_gate, w_up, w_down
        )
    rows = COLUMNS * local * PLACES * CAP
    part = PLACES * CAP
    bf16, f32 = jnp.bfloat16, jnp.float32

    def along(value):
        far = [swap(value, "inner", PLACES, 2 * z) for z in (2, 3, 1)]
        return [value, far[2], far[0], far[1]]

    def both(near):
        return [one for z in near for one in (z, swap(z, "inner", PLACES, 1))]

    def exchange(pieces):
        return [pieces[0]] + [swap(pieces[m], "group", COLUMNS, m) for m in (1, 2, 3)]

    def loaded(weight, name):
        return pl.pallas_call(
            load_kernel,
            name=name,
            out_shape=pltpu.VMEM(weight.shape, bf16),
            in_specs=[pl.BlockSpec(memory_space=pltpu.HBM)],
            out_specs=whole(),
            scratch_shapes=[pltpu.SemaphoreType.DMA],
            compiler_params=params(8),
            cost_estimate=cost(0, 2 * weight.size * 2),
        )(pltpu.with_memory_space_constraint(weight, pltpu.HBM))

    full_width = 2 * width + TABLE
    own = pl.pallas_call(
        pack_kernel,
        name="pack",
        grid=(1,),
        out_shape=jax.ShapeDtypeStruct((count, full_width), bf16),
        in_specs=[
            pl.BlockSpec((count, width), lambda n: (0, 0)),
            pl.BlockSpec((count, width), lambda n: (0, 0)),
            pl.BlockSpec((GLIMIT, count), lambda n: (0, 0)),
            pl.BlockSpec((GLIMIT, TOPK // GLIMIT, count), lambda n: (0, 0, 0)),
            pl.BlockSpec((TOPK, count), lambda n: (0, 0)),
        ],
        out_specs=pl.BlockSpec((count, full_width), lambda n: (0, 0)),
        compiler_params=params(8, 1),
    )(
        *(
            pltpu.with_memory_space_constraint(value, pltpu.HBM)
            for value in (tokens, upstream, group_choice.T, pair_pick.transpose(1, 2, 0), gate_weights.T)
        )
    )
    near = along(own)
    held_gate = loaded(w_gate, "load_gate")
    held_up = loaded(w_up, "load_up")
    held_down = loaded(w_down, "load_down")
    *far, held_gate, held_up = lax.optimization_barrier((*near[2:], held_gate, held_up))
    near = near[:2] + far

    sent = [jax.ShapeDtypeStruct((local, part, width), bf16)] * COLUMNS
    square = jax.ShapeDtypeStruct((rows, rows), bf16)
    place = jnp.stack([lax.axis_index("group"), lax.axis_index("inner")]).astype(jnp.int32)
    *sends, pick_t, high, low = pl.pallas_call(
        functools.partial(select_kernel, local, count),
        name="select",
        out_shape=sent + sent + [square] * 3,
        in_specs=[pl.BlockSpec(memory_space=pltpu.SMEM)] + [whole()] * PLACES,
        out_specs=[whole()] * (2 * COLUMNS + 3),
        scratch_shapes=[pltpu.VMEM((PLACES * count, 2 * width), bf16)],
        compiler_params=params(16),
        cost_estimate=cost(4 * rows * rows * width, 8 * rows * width),
    )(place, *both(near))
    x_recv = exchange(sends[:COLUMNS])
    dy_recv = exchange(sends[COLUMNS:])

    hid = lambda t: jax.ShapeDtypeStruct((local, rows // local, hidden), t)
    weight_bytes = 2 * local * width * hidden
    flops = 2 * rows * width * hidden

    g, u, h, *out_send = pl.pallas_call(
        forward_kernel,
        name="forward",
        out_shape=[hid(f32), hid(f32), hid(bf16)] + sent,
        in_specs=[whole()] * (COLUMNS + 3),
        out_specs=[whole()] * (COLUMNS + 3),
        compiler_params=params(8),
        cost_estimate=cost(12 * flops, 3 * weight_bytes),
    )(*x_recv, held_gate, held_up, held_down)
    out_back = exchange(out_send)

    dg, du, *dx_send = pl.pallas_call(
        backward_kernel,
        name="backward",
        out_shape=[hid(bf16), hid(bf16)] + sent,
        in_specs=[whole()] * (COLUMNS + 5),
        out_specs=[whole()] * (COLUMNS + 2),
        compiler_params=params(8),
        cost_estimate=cost(12 * flops, 3 * weight_bytes),
    )(*dy_recv, g, u, held_gate, held_up, held_down)
    dx_back = exchange(dx_send)

    def combine(blends, pieces, name):
        half = jax.ShapeDtypeStruct((PLACES // 2, count, width), bf16)
        even, odd = pl.pallas_call(
            functools.partial(combine_kernel, count, len(blends)),
            name=name,
            out_shape=[half, half],
            in_specs=[whole()] * (len(blends) + COLUMNS),
            out_specs=[whole()] * 2,
            scratch_shapes=[pltpu.VMEM((rows, width), bf16)],
            compiler_params=params(8),
            cost_estimate=cost(2 * rows * rows * width, 4 * rows * width),
        )(*blends, *pieces)
        other = swap(odd, "inner", PLACES, 1)
        sums = [even[z].astype(f32) + other[z].astype(f32) for z in range(PLACES // 2)]
        return sums[0], [sums[z].astype(bf16) for z in (1, 2, 3)]

    def finish(total, parts):
        for z in (1, 2, 3):
            total = total + swap(parts[z - 1], "inner", PLACES, 2 * z).astype(f32)
        return total.astype(bf16)

    slot_spec = pl.BlockSpec((1, part, width), lambda e: (e, 0, 0))
    hid_spec = pl.BlockSpec((1, rows // local, hidden), lambda e: (e, 0, 0))
    up_spec = pl.BlockSpec((1, 1, width, hidden), lambda e: (0, e, 0, 0))
    down_spec = pl.BlockSpec((1, 1, hidden, width), lambda e: (0, e, 0, 0))

    out_own, out_parts = combine([high, low], [after(out_back[0], *dx_send)] + out_back[1:], "combine_out")
    mixed = finish(out_own, out_parts)
    grad_down = pl.pallas_call(
        down_grads_kernel,
        name="down_grads",
        grid=(local,),
        out_shape=jax.ShapeDtypeStruct(w_down.shape, bf16),
        in_specs=[slot_spec] * COLUMNS + [hid_spec],
        out_specs=down_spec,
        compiler_params=params(32, 1),
        cost_estimate=cost(4 * flops, weight_bytes),
    )(*dy_recv, after(h, *out_parts))

    dx_own, dx_parts = combine([pick_t], [after(dx_back[0], grad_down)] + dx_back[1:], "combine_dx")
    grad_tokens = finish(dx_own, dx_parts)
    grad_gate, grad_up = pl.pallas_call(
        up_grads_kernel,
        name="up_grads",
        grid=(local,),
        out_shape=[jax.ShapeDtypeStruct(w.shape, bf16) for w in (w_gate, w_up)],
        in_specs=[slot_spec] * COLUMNS + [hid_spec] * 2,
        out_specs=[up_spec, up_spec],
        compiler_params=params(32, 1),
        cost_estimate=cost(8 * flops, 2 * weight_bytes),
    )(*x_recv, after(dg, *dx_parts), du)
    return (mixed, grad_tokens, grad_gate, grad_up, grad_down)


def solution(mesh):
    ours = mesh.shape["group"] == COLUMNS and mesh.shape["inner"] == PLACES
    in_specs = (
        P(("group", "inner"), None),
        P(("group", "inner"), None),
        P(("group", "inner"), None),
        P(("group", "inner"), None),
        P(("group", "inner"), None, None),
        P(("group", "inner"), None, None, None),
        P(("group", "inner"), None, None, None),
        P(("group", "inner"), None, None, None),
    )
    out_specs = (
        P(("group", "inner"), None),
        P(("group", "inner"), None),
        P(("group", "inner"), None, None, None),
        P(("group", "inner"), None, None, None),
        P(("group", "inner"), None, None, None),
    )
    return jax.shard_map(
        on_device if ours else on_device_general, mesh=mesh, in_specs=in_specs, out_specs=out_specs, check_vma=False
    )
```

```python
import functools

import jax
import jax.numpy as jnp
from jax import lax
from jax.experimental import pallas as pl
from jax.experimental.pallas import tpu as pltpu
from jax.sharding import PartitionSpec as P


EXPERTS = 128
TOPK = 8
RGROUPS = 8
GLIMIT = 4
CAP = 2


def expert_ids(group_choice, pair_pick):
    per_group = EXPERTS // RGROUPS
    joined = group_choice[:, :, None] * per_group + pair_pick
    return joined.reshape(joined.shape[0], TOPK)


def slot_table(ids, weights):
    flat = ids.reshape(-1)
    number = flat.shape[0]
    onehot = (flat[:, None] == jnp.arange(EXPERTS, dtype=jnp.int32)[None, :]).astype(jnp.int32)
    before = jnp.cumsum(onehot, axis=0) - onehot
    rank = jnp.sum(before * onehot, axis=1)
    target = jnp.where(rank < CAP, flat * CAP + rank, EXPERTS * CAP)
    owner = jnp.arange(number, dtype=jnp.int32) // TOPK
    empty = ids.shape[0]
    slot_token = jnp.full((EXPERTS * CAP + 1,), empty, jnp.int32).at[target].set(owner)[:-1]
    slot_weight = (
        jnp.zeros((EXPERTS * CAP + 1,), jnp.float32).at[target].set(weights.reshape(-1))[:-1]
    )
    return (slot_token, slot_weight)


def dispatch(rows, groups, inner, split, slots, width):
    local, owners, joined = rows.shape
    copies = jnp.broadcast_to(rows[:, :, None], (local, owners, split, joined))
    copies = copies.reshape(local, groups, inner, joined)
    received = lax.all_to_all(
        lax.all_to_all(copies, "group", split_axis=1, concat_axis=1, tiled=True),
        "inner",
        split_axis=2,
        concat_axis=2,
        tiled=True,
    )
    return received.reshape(local, groups * inner * slots, width)


def send_back(partial_value, groups, inner, split):
    local, total, width = partial_value.shape
    slots = total // (groups * inner)
    owners = groups * inner // split
    returned = lax.all_to_all(
        lax.all_to_all(
            partial_value.reshape(local, groups, inner, slots * width).astype(jnp.bfloat16),
            "group",
            split_axis=1,
            concat_axis=1,
            tiled=True,
        ),
        "inner",
        split_axis=2,
        concat_axis=2,
        tiled=True,
    ).astype(jnp.float32)
    returned = jnp.sum(returned.reshape(local, owners, split, slots * width), axis=2).astype(
        jnp.bfloat16
    )
    return returned.reshape(local * owners * slots, width)


def on_device_general(tokens, upstream, gate_weights, group_choice, pair_pick, w_gate, w_up, w_down):
    groups = lax.axis_size("group")
    inner = lax.axis_size("inner")
    devices = groups * inner
    local = w_gate.shape[1]
    split = devices * local // EXPERTS
    owners = devices // split
    count = tokens.shape[0]
    width = tokens.shape[1]
    ids = expert_ids(group_choice, pair_pick)
    slot_token, slot_weight = slot_table(ids, gate_weights)
    order_token = slot_token.reshape(owners, local, CAP).transpose(1, 0, 2).reshape(-1)
    order_weight = slot_weight.reshape(owners, local, CAP).transpose(1, 0, 2).reshape(-1)
    filler = jnp.zeros((1, width), tokens.dtype)
    x_pad = jnp.concatenate([tokens, filler], axis=0)
    dy_pad = jnp.concatenate([upstream, filler], axis=0)
    x_rows = x_pad[order_token].reshape(local, owners, CAP * width)
    x_recv = dispatch(x_rows, groups, inner, split, CAP, width)
    w_g = w_gate[0]
    w_u = w_up[0]
    w_d = w_down[0]
    gate = jnp.einsum("lrd,ldf->lrf", x_recv, w_g, preferred_element_type=jnp.float32)
    upv = jnp.einsum("lrd,ldf->lrf", x_recv, w_u, preferred_element_type=jnp.float32)
    sig = jax.nn.sigmoid(gate)
    act = gate * sig
    hidden = (act * upv).astype(jnp.bfloat16)
    out_partial = jnp.einsum("lrf,lfd->lrd", hidden, w_d, preferred_element_type=jnp.float32)
    out_values = send_back(out_partial, groups, inner, split)
    onehot = order_token[None, :] == jnp.arange(count, dtype=jnp.int32)[:, None]
    blend = jnp.where(onehot, order_weight[None, :], 0.0)
    mixed = jnp.dot(
        blend,
        out_values.astype(jnp.float32),
        precision=lax.Precision.HIGHEST,
        preferred_element_type=jnp.float32,
    ).astype(jnp.bfloat16)
    dout_rows = (order_weight[:, None] * dy_pad[order_token].astype(jnp.float32)).astype(
        jnp.bfloat16
    )
    dout = dispatch(dout_rows.reshape(local, owners, CAP * width), groups, inner, split, CAP, width)
    dh = jnp.einsum("lrd,lfd->lrf", dout, w_d, preferred_element_type=jnp.float32)
    dgate = (dh * upv * sig * (1.0 + gate * (1.0 - sig))).astype(jnp.bfloat16)
    dup = (dh * act).astype(jnp.bfloat16)
    dx_partial = jnp.einsum(
        "lrf,ldf->lrd", dgate, w_g, preferred_element_type=jnp.float32
    ) + jnp.einsum("lrf,ldf->lrd", dup, w_u, preferred_element_type=jnp.float32)
    grad_gate = jnp.einsum(
        "lrd,lrf->ldf", x_recv, dgate, preferred_element_type=jnp.float32
    ).astype(jnp.bfloat16)
    grad_up = jnp.einsum("lrd,lrf->ldf", x_recv, dup, preferred_element_type=jnp.float32).astype(
        jnp.bfloat16
    )
    grad_down = jnp.einsum("lrf,lrd->lfd", hidden, dout, preferred_element_type=jnp.float32).astype(
        jnp.bfloat16
    )
    dx_values = send_back(dx_partial, groups, inner, split)
    select = onehot.astype(jnp.bfloat16)
    grad_tokens = jnp.dot(select, dx_values, preferred_element_type=jnp.float32).astype(
        jnp.bfloat16
    )
    return (mixed, grad_tokens, grad_gate[None], grad_up[None], grad_down[None])


COLUMNS = 4
PLACES = 8
TABLE = 128
MIB = 1024 * 1024


def params(mib, rank=0):
    return pltpu.CompilerParams(
        vmem_limit_bytes=mib * MIB,
        dimension_semantics=("arbitrary",) * rank if rank else None,
    )


def cost(flops, moved):
    return pl.CostEstimate(flops=int(flops), bytes_accessed=int(moved), transcendentals=0)


def swap(value, axis, size, mask):
    return lax.ppermute(value, axis, [(k, k ^ mask) for k in range(size)])


def whole():
    return pl.BlockSpec(memory_space=pltpu.VMEM)


def pack_kernel(tokens_ref, upstream_ref, choice_ref, pick_ref, weight_ref, packed_ref):
    count, width = tokens_ref.shape
    per_group = EXPERTS // RGROUPS
    parts = []
    for k in range(TOPK):
        group, place = choice_ref[k // 2 : k // 2 + 1, :], pick_ref[k // 2, k % 2 : k % 2 + 1, :]
        parts.append((group * per_group + place).astype(jnp.float32))
    left = weight_ref[...]
    for _ in range(3):
        high = left.astype(jnp.bfloat16).astype(jnp.float32)
        parts.append(high)
        left = left - high
    parts.append(jnp.zeros((TABLE - 4 * TOPK, count), jnp.float32))
    packed_ref[:, :width] = tokens_ref[...]
    packed_ref[:, width : 2 * width] = upstream_ref[...]
    packed_ref[:, 2 * width :] = jnp.concatenate(parts, axis=0).T.astype(jnp.bfloat16)


def select_kernel(local, count, place_ref, *refs):
    pieces, rest = refs[:PLACES], refs[PLACES:]
    x_outs, dy_outs, rest = rest[:COLUMNS], rest[COLUMNS : 2 * COLUMNS], rest[2 * COLUMNS :]
    pick_t_ref, high_ref, low_ref, full = rest
    width = full.shape[1] // 2
    total = PLACES * count
    rows = COLUMNS * local * PLACES * CAP
    for j in range(PLACES):
        full[j * count : (j + 1) * count, :] = pieces[j][:, : full.shape[1]]
    table = jnp.concatenate([piece[:, full.shape[1] :].astype(jnp.float32) for piece in pieces], axis=0).T
    row = lax.broadcasted_iota(jnp.int32, (rows, 1), 0)
    slot = row % CAP
    piece = row // CAP % PLACES
    column = place_ref[0] ^ (row // (CAP * PLACES * local))
    expert = (column * PLACES + place_ref[1]) * local + row // (CAP * PLACES) % local
    expert = expert.astype(jnp.float32)
    member = jnp.zeros((rows, total), jnp.float32)
    weight = jnp.zeros((rows, total), jnp.float32)
    for k in range(TOPK):
        same = table[k : k + 1, :] == expert
        member = jnp.where(same, 1.0, member)
        value = table[TOPK + k : TOPK + k + 1, :] + table[2 * TOPK + k : 2 * TOPK + k + 1, :]
        value = value + table[3 * TOPK + k : 3 * TOPK + k + 1, :]
        weight = jnp.where(same, value, weight)
    other = lax.broadcasted_iota(jnp.int32, (total, 1), 0)
    token = lax.broadcasted_iota(jnp.int32, (1, total), 1)
    earlier = ((other < token) & (other // count == token // count)).astype(jnp.float32)
    rank = jnp.dot(
        member.astype(jnp.bfloat16), earlier.astype(jnp.bfloat16), preferred_element_type=jnp.float32
    )
    kept = (member > 0.5) & (rank == slot.astype(jnp.float32)) & (token // count == piece)
    pick = jnp.where(kept, 1.0, 0.0)
    weight = jnp.where(kept, weight, 0.0)
    scale = jnp.sum(weight, axis=1, keepdims=True)
    chosen = jnp.dot(pick.astype(jnp.bfloat16), full[...], preferred_element_type=jnp.float32)
    x_rows = chosen[:, :width].astype(jnp.bfloat16)
    dy_rows = (chosen[:, width:] * scale).astype(jnp.bfloat16)
    part = rows // COLUMNS
    for m in range(COLUMNS):
        x_outs[m][...] = x_rows[m * part : (m + 1) * part].reshape(x_outs[m].shape)
        dy_outs[m][...] = dy_rows[m * part : (m + 1) * part].reshape(dy_outs[m].shape)
    pick_t_ref[...] = pick.T.astype(jnp.bfloat16)
    weight = weight.T
    high = weight.astype(jnp.bfloat16)
    high_ref[...] = high
    low_ref[...] = (weight - high.astype(jnp.float32)).astype(jnp.bfloat16)


def combine_kernel(count, terms, *refs):
    blends, pieces, (even_ref, odd_ref, full) = refs[:terms], refs[terms : terms + COLUMNS], refs[terms + COLUMNS :]
    width = full.shape[1]
    part = full.shape[0] // COLUMNS
    for m in range(COLUMNS):
        full[m * part : (m + 1) * part, :] = pieces[m][...].reshape(part, width)
    value = jnp.dot(blends[0][...], full[...], preferred_element_type=jnp.float32)
    for blend in blends[1:]:
        value = value + jnp.dot(blend[...], full[...], preferred_element_type=jnp.float32)
    value = value.astype(jnp.bfloat16)
    for j in range(PLACES):
        target = odd_ref if j % 2 else even_ref
        target[j // 2] = value[j * count : (j + 1) * count]


def across(a, b):
    return lax.dot_general(a, b, (((1,), (1,)), ((), ())), preferred_element_type=jnp.float32)


def down(a, b):
    return lax.dot_general(a, b, (((0,), (0,)), ((), ())), preferred_element_type=jnp.float32)


def joined(pieces, e):
    return jnp.concatenate([piece[e] for piece in pieces], axis=0)


def load_kernel(source_ref, held_ref, done):
    copy = pltpu.make_async_copy(source_ref, held_ref, done)
    copy.start()
    copy.wait()


def forward_kernel(*refs):
    pieces = refs[:COLUMNS]
    wg_ref, wu_ref, wd_ref, g_ref, u_ref, h_ref = refs[COLUMNS : COLUMNS + 6]
    outs = refs[COLUMNS + 6 :]
    part = outs[0].shape[1]

    @pl.loop(0, wg_ref.shape[1])
    def _(e):
        rows = joined(pieces, e)
        g = jnp.dot(rows, wg_ref[0, e], preferred_element_type=jnp.float32)
        u = jnp.dot(rows, wu_ref[0, e], preferred_element_type=jnp.float32)
        h = (g * jax.nn.sigmoid(g) * u).astype(jnp.bfloat16)
        g_ref[e] = g
        u_ref[e] = u
        h_ref[e] = h
        value = jnp.dot(h, wd_ref[0, e], preferred_element_type=jnp.float32).astype(jnp.bfloat16)
        for m in range(COLUMNS):
            outs[m][e] = value[m * part : (m + 1) * part]


def backward_kernel(*refs):
    pieces = refs[:COLUMNS]
    g_ref, u_ref, wg_ref, wu_ref, wd_ref, dg_ref, du_ref = refs[COLUMNS : COLUMNS + 7]
    outs = refs[COLUMNS + 7 :]
    part = outs[0].shape[1]

    @pl.loop(0, wg_ref.shape[1])
    def _(e):
        dh = across(joined(pieces, e), wd_ref[0, e])
        g = g_ref[e]
        sig = jax.nn.sigmoid(g)
        dg = (dh * u_ref[e] * sig * (1.0 + g * (1.0 - sig))).astype(jnp.bfloat16)
        du = (dh * (g * sig)).astype(jnp.bfloat16)
        dg_ref[e] = dg
        du_ref[e] = du
        value = (across(dg, wg_ref[0, e]) + across(du, wu_ref[0, e])).astype(jnp.bfloat16)
        for m in range(COLUMNS):
            outs[m][e] = value[m * part : (m + 1) * part]


def up_grads_kernel(*refs):
    pieces = refs[:COLUMNS]
    dg_ref, du_ref, gg_ref, gu_ref = refs[COLUMNS:]
    rows = joined(pieces, 0)
    gg_ref[0, 0] = down(rows, dg_ref[0]).astype(jnp.bfloat16)
    gu_ref[0, 0] = down(rows, du_ref[0]).astype(jnp.bfloat16)


def down_grads_kernel(*refs):
    pieces = refs[:COLUMNS]
    h_ref, gd_ref = refs[COLUMNS:]
    gd_ref[0, 0] = down(h_ref[0], joined(pieces, 0)).astype(jnp.bfloat16)


def after(value, *others):
    return lax.optimization_barrier((value, *others))[0]


def on_device(tokens, upstream, gate_weights, group_choice, pair_pick, w_gate, w_up, w_down):
    count, width = tokens.shape
    local, hidden = w_gate.shape[1], w_gate.shape[3]
    if COLUMNS * PLACES * local != EXPERTS or local * PLACES * CAP != 2 * count:
        return on_device_general(
            tokens, upstream, gate_weights, group_choice, pair_pick, w_gate, w_up, w_down
        )
    rows = COLUMNS * local * PLACES * CAP
    part = PLACES * CAP
    bf16, f32 = jnp.bfloat16, jnp.float32

    def along(value):
        far = [swap(value, "inner", PLACES, 2 * z) for z in (2, 3, 1)]
        return [value, far[2], far[0], far[1]]

    def both(near):
        return [one for z in near for one in (z, swap(z, "inner", PLACES, 1))]

    def exchange(pieces):
        return [pieces[0]] + [swap(pieces[m], "group", COLUMNS, m) for m in (1, 2, 3)]

    def loaded(weight, name):
        return pl.pallas_call(
            load_kernel,
            name=name,
            out_shape=pltpu.VMEM(weight.shape, bf16),
            in_specs=[pl.BlockSpec(memory_space=pltpu.HBM)],
            out_specs=whole(),
            scratch_shapes=[pltpu.SemaphoreType.DMA],
            compiler_params=params(8),
            cost_estimate=cost(0, 2 * weight.size * 2),
        )(pltpu.with_memory_space_constraint(weight, pltpu.HBM))

    full_width = 2 * width + TABLE
    own = pl.pallas_call(
        pack_kernel,
        name="pack",
        grid=(1,),
        out_shape=jax.ShapeDtypeStruct((count, full_width), bf16),
        in_specs=[
            pl.BlockSpec((count, width), lambda n: (0, 0)),
            pl.BlockSpec((count, width), lambda n: (0, 0)),
            pl.BlockSpec((GLIMIT, count), lambda n: (0, 0)),
            pl.BlockSpec((GLIMIT, TOPK // GLIMIT, count), lambda n: (0, 0, 0)),
            pl.BlockSpec((TOPK, count), lambda n: (0, 0)),
        ],
        out_specs=pl.BlockSpec((count, full_width), lambda n: (0, 0)),
        compiler_params=params(8, 1),
    )(
        *(
            pltpu.with_memory_space_constraint(value, pltpu.HBM)
            for value in (tokens, upstream, group_choice.T, pair_pick.transpose(1, 2, 0), gate_weights.T)
        )
    )
    near = along(own)
    held_gate = loaded(w_gate, "load_gate")
    held_up = loaded(w_up, "load_up")
    held_down = loaded(w_down, "load_down")
    *far, held_gate, held_up = lax.optimization_barrier((*near[2:], held_gate, held_up))
    near = near[:2] + far

    sent = [jax.ShapeDtypeStruct((local, part, width), bf16)] * COLUMNS
    square = jax.ShapeDtypeStruct((rows, rows), bf16)
    place = jnp.stack([lax.axis_index("group"), lax.axis_index("inner")]).astype(jnp.int32)
    *sends, pick_t, high, low = pl.pallas_call(
        functools.partial(select_kernel, local, count),
        name="select",
        out_shape=sent + sent + [square] * 3,
        in_specs=[pl.BlockSpec(memory_space=pltpu.SMEM)] + [whole()] * PLACES,
        out_specs=[whole()] * (2 * COLUMNS + 3),
        scratch_shapes=[pltpu.VMEM((PLACES * count, 2 * width), bf16)],
        compiler_params=params(16),
        cost_estimate=cost(4 * rows * rows * width, 8 * rows * width),
    )(place, *both(near))
    x_recv = exchange(sends[:COLUMNS])
    dy_recv = exchange(sends[COLUMNS:])

    hid = lambda t: jax.ShapeDtypeStruct((local, rows // local, hidden), t)
    weight_bytes = 2 * local * width * hidden
    flops = 2 * rows * width * hidden

    g, u, h, *out_send = pl.pallas_call(
        forward_kernel,
        name="forward",
        out_shape=[hid(f32), hid(f32), hid(bf16)] + sent,
        in_specs=[whole()] * (COLUMNS + 3),
        out_specs=[whole()] * (COLUMNS + 3),
        compiler_params=params(8),
        cost_estimate=cost(12 * flops, 3 * weight_bytes),
    )(*x_recv, held_gate, held_up, held_down)
    out_back = exchange(out_send)

    dg, du, *dx_send = pl.pallas_call(
        backward_kernel,
        name="backward",
        out_shape=[hid(bf16), hid(bf16)] + sent,
        in_specs=[whole()] * (COLUMNS + 5),
        out_specs=[whole()] * (COLUMNS + 2),
        compiler_params=params(8),
        cost_estimate=cost(12 * flops, 3 * weight_bytes),
    )(*dy_recv, g, u, held_gate, held_up, held_down)
    dx_back = exchange(dx_send)

    def combine(blends, pieces, name):
        half = jax.ShapeDtypeStruct((PLACES // 2, count, width), bf16)
        even, odd = pl.pallas_call(
            functools.partial(combine_kernel, count, len(blends)),
            name=name,
            out_shape=[half, half],
            in_specs=[whole()] * (len(blends) + COLUMNS),
            out_specs=[whole()] * 2,
            scratch_shapes=[pltpu.VMEM((rows, width), bf16)],
            compiler_params=params(8),
            cost_estimate=cost(2 * rows * rows * width, 4 * rows * width),
        )(*blends, *pieces)
        other = swap(odd, "inner", PLACES, 1)
        sums = [even[z].astype(f32) + other[z].astype(f32) for z in range(PLACES // 2)]
        return sums[0], [sums[z].astype(bf16) for z in (1, 2, 3)]

    def finish(total, parts):
        for z in (3, 2, 1):
            total = total + swap(parts[z - 1], "inner", PLACES, 2 * z).astype(f32)
        return total.astype(bf16)

    slot_spec = pl.BlockSpec((1, part, width), lambda e: (e, 0, 0))
    hid_spec = pl.BlockSpec((1, rows // local, hidden), lambda e: (e, 0, 0))
    up_spec = pl.BlockSpec((1, 1, width, hidden), lambda e: (0, e, 0, 0))
    down_spec = pl.BlockSpec((1, 1, hidden, width), lambda e: (0, e, 0, 0))

    out_own, out_parts = combine([high, low], [after(out_back[0], *dx_send)] + out_back[1:], "combine_out")
    mixed = finish(out_own, out_parts)
    grad_down = pl.pallas_call(
        down_grads_kernel,
        name="down_grads",
        grid=(local,),
        out_shape=jax.ShapeDtypeStruct(w_down.shape, bf16),
        in_specs=[slot_spec] * COLUMNS + [hid_spec],
        out_specs=down_spec,
        compiler_params=params(32, 1),
        cost_estimate=cost(4 * flops, weight_bytes),
    )(*dy_recv, after(h, *out_parts))

    dx_own, dx_parts = combine([pick_t], [after(dx_back[0], grad_down)] + dx_back[1:], "combine_dx")
    grad_tokens = finish(dx_own, dx_parts)
    grad_gate, grad_up = pl.pallas_call(
        up_grads_kernel,
        name="up_grads",
        grid=(local,),
        out_shape=[jax.ShapeDtypeStruct(w.shape, bf16) for w in (w_gate, w_up)],
        in_specs=[slot_spec] * COLUMNS + [hid_spec] * 2,
        out_specs=[up_spec, up_spec],
        compiler_params=params(32, 1),
        cost_estimate=cost(8 * flops, 2 * weight_bytes),
    )(*x_recv, after(dg, *dx_parts), du)
    return (mixed, grad_tokens, grad_gate, grad_up, grad_down)


def solution(mesh):
    ours = mesh.shape["group"] == COLUMNS and mesh.shape["inner"] == PLACES
    in_specs = (
        P(("group", "inner"), None),
        P(("group", "inner"), None),
        P(("group", "inner"), None),
        P(("group", "inner"), None),
        P(("group", "inner"), None, None),
        P(("group", "inner"), None, None, None),
        P(("group", "inner"), None, None, None),
        P(("group", "inner"), None, None, None),
    )
    out_specs = (
        P(("group", "inner"), None),
        P(("group", "inner"), None),
        P(("group", "inner"), None, None, None),
        P(("group", "inner"), None, None, None),
        P(("group", "inner"), None, None, None),
    )
    return jax.shard_map(
        on_device if ours else on_device_general, mesh=mesh, in_specs=in_specs, out_specs=out_specs, check_vma=False
    )
```
